32 devices in a mesh: exp: 8 (over z, x), tp: 4 (over y, core).
Axes of the slice: x: 2, y: 2, z: 4, core: 2. Of those that a mesh axis runs over, the one named last changes fastest.
Arguments:
- tokens: bfloat16 [2048, 3584], P('exp', 'tp'), may hold values from -6 to 6
- cotangent: bfloat16 [2048, 3584], P('exp', 'tp'), may hold values from -3 to 3
- up_weight: bfloat16 [8, 3584, 2432], P('exp', None, 'tp'), may hold values from -0.09375 to 0.09375
- down_weight: bfloat16 [8, 2432, 3584], P('exp', 'tp'), may hold values from -0.125 to 0.125
- expert_ids: int32 [2048, 2], P('exp'), may hold values from 0 to 7, all different within a row; in each aligned block of 256 rows (0 to 255, 256 to 511, ...) at most 128 rows name the same one
- gate_probs: bfloat16 [2048, 2], P('exp'), may hold values from 0.049804688 to 0.94921875
Outputs:
- token_grad: bfloat16 [2048, 3584], P('exp', 'tp')
- up_grad: bfloat16 [8, 3584, 2432], P('exp', None, 'tp')
- down_grad: bfloat16 [8, 2432, 3584], P('exp', 'tp')
The draws below stay inside these ranges and needn't reach their ends.
Inputs may be any that keep to these rules, and one draw needn't show every extreme that they name: `expert_ids`: each row names 2 different experts. Among the 256 rows of one index of exp no expert is named more than 128 times, a bound that some block reaches.
All inputs are finite; a program needn't handle non-finite values.
Results may differ from the reference program's by a relative error of at most 0.019.
Values may be sent and summed in bfloat16 or wider, within the bound.
No kernel may reach another device: no remote copies, remote signals or barrier semaphores. Data moves between devices by JAX's collectives and lax.ppermute only.
A program may use at most 128 MiB of HBM per device.

```python
import math
import jax
import jax.numpy as jnp
import numpy as np
from jax import lax

D = 3584
FF = 2432
TOP = 2
TOK_DEV = 256
EXPERTS = 8
TOKENS = 2048
SLOT = 128
CAP = 640
N_TP = 4


def block_levels(rng, shape, pieces, smallest, largest):
    gain = 1.0
    for dim, shards_of in pieces:
        steps = jax.random.uniform(jax.random.fold_in(jax.random.fold_in(rng, 6), dim), (shards_of,), jnp.float32, smallest / len(pieces), largest / len(pieces))
        gain = gain * jnp.repeat(jnp.exp(steps), shape[dim] // shards_of).reshape((-1,) + (1,) * (len(shape) - 1 - dim))
    return gain


def shared_out(rng, own, number, rows, count, top, reach, skew):
    ranking = jax.random.permutation(rng, count)
    crowded, common = shares(count, rows * top, reach, skew, True), shares(count, rows * top, reach, skew, False)
    places = jnp.arange(count)

    def named(lengths, turn):
        used = int((lengths > 0).sum())
        fixed = max(1, used // 4)
        moved = fixed + (places - fixed + turn * (used - fixed)) % max(1, count - fixed)
        return jnp.zeros((count,), jnp.int32).at[ranking[jnp.where(places < fixed, places, moved)]].set(jnp.asarray(lengths, jnp.int32))

    lengths = jnp.where(number % 4 == 0, named(crowded, number // 4), named(common, number - number // 4 - 1))
    mixed = jax.random.permutation(jax.random.fold_in(own, 3), count)
    giver, receiver = mixed[0:count // 2 * 2:2], mixed[1:count // 2 * 2:2]
    room = jnp.minimum(lengths[giver] - 1, reach - lengths[receiver]) // 2
    room = jnp.where((giver == ranking[0]) | (receiver == ranking[0]) | (lengths[receiver] == 0), 0, jnp.maximum(room, 0))
    moved = jax.random.randint(jax.random.fold_in(own, 4), (count // 2,), 0, 1 << 20) % (room + 1)
    lengths = lengths.at[giver].add(-moved).at[receiver].add(moved)
    items = jnp.searchsorted(jnp.cumsum(lengths), jnp.arange(rows * top), side="right").astype(jnp.int32)
    grid = items.reshape(top, rows).T
    grid = grid[jax.random.permutation(jax.random.fold_in(own, 1), rows)]
    turn = jax.random.randint(jax.random.fold_in(own, 2), (rows, 1), 0, top)
    return jnp.take_along_axis(grid, (jnp.arange(top)[None, :] + turn) % top, axis=1)


def shares(number_of, total, most, skew, full):
    loads = [(1 << 20) // math.isqrt(rank ** skew) + 1 for rank in range(1, number_of + 1)]
    largest = most if full else min(most, max(-(-total // number_of), total * loads[0] // sum(loads)))
    least = 1 if total - largest >= number_of - 1 else 0
    given, rest = [largest] + [least] * (number_of - 1), total - largest - least * (number_of - 1)
    while rest > 0:
        candidates = [i for i in range(1, number_of) if given[i] < largest] or [i for i in range(1, number_of) if given[i] < most]
        whole, left = sum([loads[i] for i in candidates]), rest
        for i in candidates:
            addition = min(most - given[i], max(1, left * loads[i] // whole), rest)
            given[i] = given[i] + addition
            rest = rest - addition
    return np.array(given)


def gaussian(rng, dims, width, bound, pieces=(), kind=jnp.bfloat16):
    values = width * jax.random.normal(rng, dims, jnp.float32)
    if pieces:
        values = values * block_levels(rng, dims, pieces, -0.22, 0.18)
    return jnp.clip(values, -bound, bound).astype(kind)


def setup_inputs(seed: int = 0) -> dict:
    arg_keys = jax.random.split(jax.random.key(seed), 7)
    tokens = gaussian(arg_keys[0], (TOKENS, D), 1.0, 6.0, ((0, 8), (1, 4)))
    cotangent = gaussian(arg_keys[1], (TOKENS, D), 0.5, 3.0, ((0, 8), (1, 4)))
    up_weight = gaussian(arg_keys[2], (EXPERTS, D, FF), D ** -0.5, 0.09375, ((0, 8), (2, 4)))
    down_weight = gaussian(arg_keys[3], (EXPERTS, FF, D), FF ** -0.5, 0.125, ((0, 8), (1, 4)))
    expert_ids_keys = jax.random.split(jax.random.fold_in(arg_keys[4], 1), TOKENS // TOK_DEV)
    expert_ids_turns = jax.random.permutation(jax.random.fold_in(arg_keys[4], 3), TOKENS // TOK_DEV)
    expert_ids = jax.vmap(lambda own, number: shared_out(jax.random.fold_in(arg_keys[4], 2), own, number, TOK_DEV, EXPERTS, TOP, SLOT, 2))(expert_ids_keys, expert_ids_turns).reshape((TOKENS, TOP))
    gate_probs = jnp.clip(0.049804688 + 0.89941406 * jax.random.uniform(arg_keys[5], (TOKENS, TOP), jnp.float32) ** block_levels(arg_keys[5], (TOKENS, TOP), ((0, 8),), -0.2, 0.2), 0.049804688, 0.94921875).astype(jnp.bfloat16)
    return dict(tokens=tokens, cotangent=cotangent, up_weight=up_weight, down_weight=down_weight, expert_ids=expert_ids, gate_probs=gate_probs)


def silu_parts(hidden):
    sigma = jax.nn.sigmoid(hidden)
    return hidden * sigma, sigma * (1.0 + hidden * (1.0 - sigma))


def reference(tokens, cotangent, up_weight, down_weight, expert_ids, gate_probs):
    flat_ids = expert_ids.reshape(-1).astype(jnp.int32)
    pairs = flat_ids.shape[0]
    onehot = (flat_ids[:, None] == jnp.arange(EXPERTS, dtype=jnp.int32)[None, :]).astype(jnp.int32)
    ranks = jnp.sum(onehot * (jnp.cumsum(onehot, axis=0) - 1), axis=1).astype(jnp.int32)
    keep = ranks < CAP
    target = jnp.where(keep, flat_ids * CAP + ranks, EXPERTS * CAP).astype(jnp.int32)
    source = jnp.zeros((EXPERTS * CAP + 1,), jnp.int32).at[target].set(jnp.arange(pairs, dtype=jnp.int32))
    filled = jnp.zeros((EXPERTS * CAP + 1,), jnp.int32).at[target].set(1)
    source = source[:-1].reshape(EXPERTS, CAP)
    filled = filled[:-1].reshape(EXPERTS, CAP)
    flat_probs = gate_probs.reshape(-1)
    block = FF // N_TP

    def one_expert(operands):
        rows, live, w_up, w_down = operands
        token_rows = (rows // TOP).astype(jnp.int32)
        alive = live > 0
        inputs = jnp.where(alive[:, None], tokens[token_rows], jnp.zeros_like(tokens[:1]))
        weights = jnp.where(alive, flat_probs[rows].astype(jnp.float32), jnp.float32(0.0))
        routed = (weights[:, None] * cotangent[token_rows].astype(jnp.float32)).astype(jnp.bfloat16)
        hidden = jnp.dot(inputs, w_up, preferred_element_type=jnp.float32)
        act_full, slope = silu_parts(hidden)
        act = act_full.astype(jnp.bfloat16)
        d_act = lax.dot_general(routed, w_down, (((1,), (1,)), ((), ())), preferred_element_type=jnp.float32)
        d_hidden = (d_act * slope).astype(jnp.bfloat16)
        grad_up = lax.dot_general(inputs, d_hidden, (((0,), (0,)), ((), ())), preferred_element_type=jnp.float32).astype(jnp.bfloat16)
        grad_down = lax.dot_general(act, routed, (((0,), (0,)), ((), ())), preferred_element_type=jnp.float32).astype(jnp.bfloat16)
        total = jnp.zeros((CAP, D), jnp.float32)
        for part in range(N_TP):
            piece = lax.dot_general(d_hidden[:, part * block:(part + 1) * block], w_up[:, part * block:(part + 1) * block], (((1,), (1,)), ((), ())), preferred_element_type=jnp.float32)
            rounded = lax.optimization_barrier(piece.astype(jnp.bfloat16))
            total = total + rounded.astype(jnp.float32)
        return grad_up, grad_down, total

    grads_up, grads_down, totals = lax.map(one_expert, (source, filled, up_weight, down_weight))
    flat_totals = jnp.concatenate([totals.reshape(EXPERTS * CAP, D), jnp.zeros((1, D), jnp.float32)], axis=0)
    per_pair = flat_totals[target]
    token_grad = jnp.sum(per_pair.reshape(TOKENS, TOP, D), axis=1).astype(jnp.bfloat16)
    return token_grad, grads_up, grads_down
```

```python
import math

import jax
import jax.numpy as jnp
from jax import lax
from jax.sharding import PartitionSpec as P

BF = jnp.bfloat16
F32 = jnp.float32


def ring_order(count):
    if count <= 4:
        return list(range(0, count, 2)) + list(range(1, count, 2))[::-1]
    return list(range(count))


class Ring:
    def __init__(self, axis, size, count, stride):
        self.axis, self.count, self.stride = axis, count, stride
        self.order = ring_order(count)
        self.half = count // 2
        spot = {c: i for i, c in enumerate(self.order)}
        self.perms = {}
        for step in (1, -1):
            pairs = []
            for index in range(size):
                c = (index // stride) % count
                there = self.order[(spot[c] + step) % count]
                pairs.append((index, index + (there - c) * stride))
            self.perms[step] = pairs
        self.spot = [spot[c] for c in range(count)]

    def send(self, value, step):
        return lax.ppermute(value, self.axis, self.perms[step])

    def coordinate(self, mine, offset):
        place = jnp.asarray(self.spot, jnp.int32)[mine]
        return jnp.asarray(self.order, jnp.int32)[(place + offset) % self.count]

    def offsets(self):
        found = [0]
        for d in range(1, self.half):
            found += [-d, d]
        return found + ([self.half] if self.count > 1 else [])

    def gather(self, value, cut):
        blocks = {0: value}
        if self.count == 2:
            blocks[1] = self.send(value, 1)
        elif self.count > 2:
            up = down = value
            for d in range(1, self.half):
                up, down = self.send(up, 1), self.send(down, -1)
                blocks[-d], blocks[d] = up, down
            blocks[self.half] = jnp.concatenate(
                [self.send(up[:cut], 1), self.send(down[cut:], -1)], axis=0
            )
        return [blocks[o] for o in self.offsets()]

    def reduce(self, blocks, cut):
        term = dict(zip(self.offsets(), blocks))
        if self.count == 1:
            return term[0]
        if self.count == 2:
            return term[0] + self.send(term[1].astype(BF), 1).astype(F32)
        up = self.send(term[self.half][:cut].astype(BF), 1).astype(F32)
        down = self.send(term[self.half][cut:].astype(BF), -1).astype(F32)
        for d in range(self.half - 1, 0, -1):
            up_sum, down_sum = term[d], term[-d]
            if d == self.half - 1:
                up_sum = jnp.concatenate([up_sum[:cut] + up, up_sum[cut:]], axis=0)
                down_sum = jnp.concatenate([down_sum[:cut], down_sum[cut:] + down], axis=0)
            else:
                up_sum, down_sum = up_sum + up, down_sum + down
            up = self.send(up_sum.astype(BF), 1).astype(F32)
            down = self.send(down_sum.astype(BF), -1).astype(F32)
        return term[0] + up + down


def pick(onehot, rows):
    return jnp.dot(onehot, rows, preferred_element_type=F32).astype(BF)


def unpick(onehot, rows):
    return lax.dot_general(onehot, rows, (((0,), (0,)), ((), ())), preferred_element_type=F32)


def silu_parts(hidden):
    sigma = jax.nn.sigmoid(hidden)
    return (hidden * sigma, sigma * (1.0 + hidden * (1.0 - sigma)))


def after(value, *others):
    return lax.optimization_barrier((value,) + others)[0]


def per_device(tokens, cotangent, up_weight, down_weight, expert_ids, gate_probs):
    tok, top = expert_ids.shape
    width = tokens.shape[1]
    n_exp, n_tp = lax.axis_size("exp"), lax.axis_size("tp")
    experts = n_exp * up_weight.shape[0]
    slot = min(4 * tok // experts, tok)
    capacity = 5 * tok * n_exp // (2 * experts)
    nx = 2 ** (int(math.log2(n_exp)) // 2)
    nz = n_exp // nx
    nc = 2 if n_tp % 2 == 0 else 1
    ny = n_tp // nc
    zring, yring, cring = (
        Ring("exp", n_exp, nz, nx),
        Ring("tp", n_tp, ny, nc),
        Ring("tp", n_tp, nc, 1),
    )
    e, t = lax.axis_index("exp"), lax.axis_index("tp")
    z, x, y, c = e // nx, e % nx, t // nc, t % nc

    def cross(value, dx):
        pairs = [(i, i // nx * nx + (i % nx + dx) % nx) for i in range(n_exp)]
        return lax.ppermute(value, "exp", pairs)

    w_up, w_down = up_weight[0], down_weight[0]
    hid = w_up.shape[1]
    first = min(-(-width // 256) * 128, width)
    edges = [(0, first), (first, width)] if first < width else [(0, width)]

    head = 16
    meta = jnp.concatenate([expert_ids.astype(BF).T, gate_probs.T], axis=0)
    meta = jnp.pad(meta, ((0, head - 2 * top), (0, edges[0][1] - tok)))

    cuts = [tok // 2] * 4
    pieces = []
    held = {}
    for source, name in ((tokens, "x"), (cotangent, "dy")):
        for k, (lo, hi) in enumerate(edges):
            pieces.append((name, k, source[:, lo:hi]))
    previous = None
    for name, k, piece in pieces:
        if name == "x" and k == 0:
            piece = jnp.concatenate([meta, piece], axis=0)
            blocks = zring.gather(piece, head + tok // 2)
            info = [b[:head, :tok] for b in blocks]
            blocks = [b[head:] for b in blocks]
        else:
            if previous is not None:
                piece = after(piece, previous)
            blocks = zring.gather(piece, tok // 2)
        previous = blocks[min(1, len(blocks) - 1)]
        held[name, k] = jnp.concatenate(blocks, axis=0)

    info = jnp.stack(info, axis=0)
    ids, probs = info[:, :top], info[:, top : 2 * top]
    rows = jnp.arange(nx, dtype=jnp.int32)
    wanted = (z * nx + (x + rows) % nx).astype(BF)
    hit = ids[None] == wanted[:, None, None, None]
    match = jnp.any(hit, axis=2)
    weight = jnp.sum(jnp.where(hit, probs[None], jnp.zeros_like(probs[None])), axis=2)
    spot = jnp.arange(tok)
    below = (spot[:, None] < spot[None, :]).astype(BF)
    local = jnp.dot(
        match.astype(BF).reshape(nx * nz, tok), below, preferred_element_type=F32
    ).astype(jnp.int32)
    local = jnp.where(match, local.reshape(nx, nz, tok), -1)
    count = jnp.sum(match.astype(F32), axis=2)

    rank_of_slot = jnp.arange(slot, dtype=jnp.int32)[:, None]
    pick_out, pick_out_w = [], []
    for dx in range(1, nx):
        onehot = local[dx][:, None, :] == rank_of_slot[None]
        pick_out.append(onehot.astype(BF))
        pick_out_w.append(jnp.where(onehot, weight[dx][:, None, :], jnp.zeros((), BF)))

    def slots(onehot, rows):
        rows = rows.reshape(nz, tok, -1)
        out = lax.dot_general(
            onehot, rows, (((2,), (1,)), ((0,), (0,))), preferred_element_type=F32
        )
        return out.astype(BF).reshape(nz * slot, -1)

    arrived = {}
    others = [count[0]]
    for name, k, _ in pieces:
        got = []
        for dx in range(1, nx):
            out = slots((pick_out if name == "x" else pick_out_w)[dx - 1], held[name, k])
            if name == "x" and k == 0:
                line = jnp.pad(count[dx][None].astype(BF), ((0, head - 1), (0, out.shape[1] - nz)))
                back = cross(jnp.concatenate([line, out], axis=0), dx)
                others.append(back[0, :nz].astype(F32))
                back = back[head:]
            else:
                back = cross(out, dx)
            got.append(back)
        arrived[name, k] = got

    zs = zring.coordinate(z, jnp.asarray(zring.offsets(), jnp.int32))
    number = jnp.stack([zs * nx + (x - dx) % nx for dx in range(nx)], axis=0)
    counts = jnp.stack(others, axis=0)
    earlier = number.reshape(-1)[None, :] < number.reshape(-1)[:, None]
    base = jnp.sum(jnp.where(earlier, counts.reshape(-1)[None, :], 0.0), axis=1)
    base = base.astype(jnp.int32).reshape(nx, nz)
    counts = counts.astype(jnp.int32)
    place = jnp.arange(capacity, dtype=jnp.int32)[:, None]
    rank = jnp.where(match[0], local[0] + base[0][:, None], -1).reshape(1, nz * tok)
    own = rank == place
    pick_own = own.astype(BF)
    pick_own_w = jnp.where(own, weight[0].reshape(1, nz * tok), jnp.zeros((), BF))
    lane = jnp.arange(slot, dtype=jnp.int32)[None, :]
    pick_in = []
    for dx in range(1, nx):
        there = jnp.where(lane < counts[dx][:, None], base[dx][:, None] + lane, -1)
        pick_in.append((there.reshape(1, nz * slot) == place).astype(BF))

    full = {}
    for name in ("x", "dy"):
        whole = jnp.zeros((capacity, n_tp * width), BF)
        for k, (lo, hi) in enumerate(edges):
            part = pick(pick_own if name == "x" else pick_own_w, held[name, k])
            for onehot, back in zip(pick_in, arrived[name, k]):
                part = part + pick(onehot, back)
            for oy, by_y in zip(yring.offsets(), yring.gather(part, capacity // 2)):
                for oc, by_c in zip(cring.offsets(), cring.gather(by_y, capacity // 2)):
                    index = yring.coordinate(y, oy) * nc + cring.coordinate(c, oc)
                    whole = lax.dynamic_update_slice(whole, by_c, (0, index * width + lo))
        full[name] = whole

    inputs, routed = full["x"], full["dy"]
    hidden = jnp.dot(inputs, w_up, preferred_element_type=F32)
    act_full, slope = silu_parts(hidden)
    act = act_full.astype(BF)
    d_act = lax.dot_general(routed, w_down, (((1,), (1,)), ((), ())), preferred_element_type=F32)
    d_hidden = (d_act * slope).astype(BF)
    grad_up = unpick(inputs, d_hidden).astype(BF)
    grad_down = unpick(act, routed).astype(BF)

    results = []
    for lo, hi in edges:
        by_y = []
        for oy in yring.offsets():
            by_c = []
            for oc in cring.offsets():
                index = yring.coordinate(y, oy) * nc + cring.coordinate(c, oc)
                part = lax.dynamic_slice(w_up, (index * width + lo, 0), (hi - lo, hid))
                by_c.append(
                    lax.dot_general(
                        d_hidden, part, (((1,), (1,)), ((), ())), preferred_element_type=F32
                    )
                )
            by_y.append(cring.reduce(by_c, capacity // 2))
        total = yring.reduce(by_y, capacity // 2).astype(BF)
        mine = unpick(pick_own, total).reshape(nz, tok, hi - lo)
        for dx in range(1, nx):
            out = unpick(pick_in[dx - 1], total).astype(BF)
            back = cross(out, -dx).reshape(nz, slot, hi - lo)
            mine = mine + lax.dot_general(
                pick_out[dx - 1], back, (((1,), (1,)), ((0,), (0,))), preferred_element_type=F32
            )
        results.append(zring.reduce([mine[i] for i in range(nz)], tok // 2).astype(BF))
    token_grad = jnp.concatenate(results, axis=1)
    return (token_grad, grad_up[None], grad_down[None])


def solution(mesh):
    placed = (
        P("exp", "tp"),
        P("exp", "tp"),
        P("exp", None, "tp"),
        P("exp", "tp", None),
        P("exp", None),
        P("exp", None),
    )
    return jax.shard_map(
        per_device,
        mesh=mesh,
        in_specs=placed,
        out_specs=(P("exp", "tp"), P("exp", None, "tp"), P("exp", "tp", None)),
        check_vma=False,
    )
```

```python
import math

import jax
import jax.numpy as jnp
from jax import lax
from jax.sharding import PartitionSpec as P

BF = jnp.bfloat16
F32 = jnp.float32
ORDER = "x0 x1 x0 x0 x1 x0 d0 x1 x0 x1 d0 d1 x1 d0 x0 d0 d1 x0 d1 d0 x1 d1 x1 d1 d0 d0 d1 d1"
FETCH = {"x": [384, 512], "d": [512, 384]}
BACK = "g0 g1 g0 g1 g0 g1 g0 g1 g0 g1 g0 g1"


def ring_order(count):
    if count <= 4:
        return list(range(0, count, 2)) + list(range(1, count, 2))[::-1]
    return list(range(count))


def lookup(table, index):
    return sum(jnp.where(index == i, jnp.int32(v), jnp.int32(0)) for i, v in enumerate(table))


class Ring:
    def __init__(self, axis, size, count, stride):
        self.axis, self.count, self.stride = axis, count, stride
        self.order = ring_order(count)
        self.half = count // 2
        spot = {c: i for i, c in enumerate(self.order)}
        self.perms = {}
        for step in (1, -1):
            pairs = []
            for index in range(size):
                c = (index // stride) % count
                there = self.order[(spot[c] + step) % count]
                pairs.append((index, index + (there - c) * stride))
            self.perms[step] = pairs
        self.spot = [spot[c] for c in range(count)]

    def send(self, value, step):
        return lax.ppermute(value, self.axis, self.perms[step])

    def coordinate(self, mine, offset):
        place = lookup(self.spot, mine)
        return lookup(self.order, lax.rem(place + offset + self.count, self.count))

    def offsets(self):
        found = [0]
        for d in range(1, self.half):
            found += [-d, d]
        return found + ([self.half] if self.count > 1 else [])

    def near(self, line, value):
        blocks = {0: value}
        up = down = value
        for d in range(1, self.half):
            up, down = self.send(up, 1), self.send(down, -1)
            yield
            up, down = line.done(up, down)
            blocks[-d], blocks[d] = up, down
        return [blocks[o] for o in self.offsets() if o in blocks]

    def far(self, line, blocks, cut):
        if self.count == 1:
            return []
        if self.count == 2:
            got = self.send(blocks[0], 1)
            yield
            return [line.done(got)]
        up, down = line.go(blocks[-2][:cut], blocks[-1][cut:])
        up, down = self.send(up, 1), self.send(down, -1)
        yield
        return [jnp.concatenate(line.done(up, down), axis=0)]

    def gather(self, line, value, cut):
        blocks = yield from self.near(line, value)
        return blocks + (yield from self.far(line, blocks, cut))

    def reduce(self, line, blocks, cut):
        term = dict(zip(self.offsets(), blocks))
        if self.count == 1:
            return term[0]
        if self.count == 2:
            got = self.send(line.go(term[1].astype(BF)), 1)
            yield
            return term[0] + line.done(got).astype(F32)
        up, down = line.go(term[self.half][:cut].astype(BF), term[self.half][cut:].astype(BF))
        up, down = self.send(up, 1), self.send(down, -1)
        yield
        for d in range(self.half - 1, 0, -1):
            up, down = line.done(up, down)
            up, down = up.astype(F32), down.astype(F32)
            up_sum, down_sum = term[d], term[-d]
            if d == self.half - 1:
                up_sum = jnp.concatenate([up_sum[:cut] + up, up_sum[cut:]], axis=0)
                down_sum = jnp.concatenate([down_sum[:cut], down_sum[cut:] + down], axis=0)
            else:
                up_sum, down_sum = up_sum + up, down_sum + down
            up, down = line.go(up_sum.astype(BF), down_sum.astype(BF))
            up, down = self.send(up, 1), self.send(down, -1)
            yield
        up, down = line.done(up, down)
        return term[0] + up.astype(F32) + down.astype(F32)


class Line:
    def __init__(self):
        self.mark = jnp.zeros((8, 128), F32)

    def go(self, *values):
        out = lax.optimization_barrier((*values, self.mark))
        return out[0] if len(values) == 1 else out[:-1]

    def done(self, *values):
        out = lax.optimization_barrier((*values, self.mark))
        self.mark = out[-1]
        return out[0] if len(values) == 1 else out[:-1]


def run(parts, order):
    results = {}

    def step(name):
        if name not in results:
            try:
                with jax.named_scope(name):
                    next(parts[name])
            except StopIteration as end:
                results[name] = end.value

    for name in order:
        step(name)
    while len(results) < len(parts):
        for name in parts:
            step(name)
    return results


def pick(onehot, rows):
    return jnp.dot(onehot, rows, preferred_element_type=F32).astype(BF)


def unpick(onehot, rows):
    return lax.dot_general(onehot, rows, (((0,), (0,)), ((), ())), preferred_element_type=F32)


def silu_parts(hidden):
    sigma = jax.nn.sigmoid(hidden)
    return (hidden * sigma, sigma * (1.0 + hidden * (1.0 - sigma)))


def per_device(tokens, cotangent, up_weight, down_weight, expert_ids, gate_probs):
    tok, top = expert_ids.shape
    width = tokens.shape[1]
    n_exp, n_tp = lax.axis_size("exp"), lax.axis_size("tp")
    experts = n_exp * up_weight.shape[0]
    slot = min(4 * tok // experts, tok)
    capacity = 5 * tok * n_exp // (2 * experts)
    nx = 2 ** (int(math.log2(n_exp)) // 2)
    nz = n_exp // nx
    nc = 2 if n_tp % 2 == 0 else 1
    ny = n_tp // nc
    zring, yring, cring = (
        Ring("exp", n_exp, nz, nx),
        Ring("tp", n_tp, ny, nc),
        Ring("tp", n_tp, nc, 1),
    )
    e, t = lax.axis_index("exp"), lax.axis_index("tp")
    z, x, y, c = lax.div(e, nx), lax.rem(e, nx), lax.div(t, nc), lax.rem(t, nc)

    def cross(value, dx):
        pairs = [(i, i // nx * nx + (i % nx + dx) % nx) for i in range(n_exp)]
        return lax.ppermute(value, "exp", pairs)

    w_up, w_down = up_weight[0], down_weight[0]
    hid = w_up.shape[1]
    first = min(-(-width // 256) * 128, width)
    edges = [(0, first), (first, width)] if first < width else [(0, width)]

    head = 16
    meta = jnp.concatenate([expert_ids.astype(BF).T, gate_probs.T], axis=0)
    meta = jnp.pad(meta, ((0, head - 2 * top), (0, (FETCH['x'][0] if width > 512 else width) - tok)))

    line = Line()
    shared = {}
    half = capacity // 2

    def ranks(info):
        info = jnp.stack(info, axis=0)
        n = info.shape[0]
        ids, probs = info[:, :top], info[:, top : 2 * top]
        shifts = jnp.arange(nx, dtype=jnp.int32)
        wanted = (z * nx + lax.rem(x + shifts, nx)).astype(BF)
        hit = ids[None] == wanted[:, None, None, None]
        match = jnp.any(hit, axis=2)
        weight = jnp.sum(jnp.where(hit, probs[None], jnp.zeros_like(probs[None])), axis=2)
        spot = jnp.arange(tok)
        below = (spot[:, None] < spot[None, :]).astype(BF)
        local = jnp.dot(
            match.astype(BF).reshape(nx * n, tok), below, preferred_element_type=F32
        ).astype(jnp.int32)
        local = jnp.where(match, local.reshape(nx, n, tok), -1)
        rank_of_slot = jnp.arange(slot, dtype=jnp.int32)[:, None]
        outs = []
        for dx in range(1, nx):
            onehot = local[dx][:, None, :] == rank_of_slot[None]
            scaled = jnp.where(onehot, weight[dx][:, None, :], jnp.zeros((), BF))
            outs.append((onehot.astype(BF), scaled))
        return dict(
            match=match[0], weight=weight[0], local=local[0], outs=outs,
            count=jnp.sum(match.astype(F32), axis=2),
        )

    def places(others):
        zs = zring.coordinate(z, jnp.asarray(zring.offsets(), jnp.int32))
        number = jnp.stack([zs * nx + lax.rem(x - dx + nx, nx) for dx in range(nx)], axis=0)
        counts = jnp.stack(others, axis=0)
        earlier = number.reshape(-1)[None, :] < number.reshape(-1)[:, None]
        base = jnp.sum(jnp.where(earlier, counts.reshape(-1)[None, :], 0.0), axis=1)
        base = base.astype(jnp.int32).reshape(nx, nz)
        counts = counts.astype(jnp.int32)
        place = jnp.arange(capacity, dtype=jnp.int32)[:, None]
        match, local, weight = (
            jnp.concatenate([g[key] for g in groups], axis=0) for key in ("match", "local", "weight")
        )
        rank = jnp.where(match, local + base[0][:, None], -1).reshape(1, nz * tok)
        own = rank == place
        shared["own"] = own.astype(BF)
        shared["own_w"] = jnp.where(own, weight.reshape(1, nz * tok), jnp.zeros((), BF))
        lane = jnp.arange(slot, dtype=jnp.int32)[None, :]
        shared["in"] = []
        for dx in range(1, nx):
            there = jnp.where(lane < counts[dx][:, None], base[dx][:, None] + lane, -1)
            shared["in"].append((there.reshape(1, nz * slot) == place).astype(BF))
        shared["out"] = [
            jnp.concatenate([g["outs"][dx - 1][0] for g in groups], axis=0) for dx in range(1, nx)
        ]

    groups = []

    def leave(group, blocks, tail, lead):
        n = len(blocks)
        rows = jnp.stack(blocks, axis=0)
        backs = []
        for dx in range(1, nx):
            onehot = group["outs"][dx - 1][1 if tail else 0]
            out = lax.dot_general(
                onehot, rows, (((2,), (1,)), ((0,), (0,))), preferred_element_type=F32
            )
            out = out.astype(BF).reshape(n * slot, -1)
            if lead:
                tally = group["count"][dx][None].astype(BF)
                tally = jnp.pad(tally, ((0, head - 1), (0, out.shape[1] - n)))
                out = jnp.concatenate([tally, out], axis=0)
            backs.append(cross(line.go(out), dx))
        return backs

    def fetch(source, lo, hi, tail, lead):
        piece = source[:, lo:hi]
        if lead:
            piece = jnp.concatenate([meta, piece], axis=0)
        piece = line.go(piece)
        top_rows = head if lead else 0
        blocks = yield from zring.near(line, piece)
        far = zring.far(line, blocks, top_rows + tok // 2)
        opposite = []
        try:
            next(far)
        except StopIteration as end:
            opposite = end.value
        yield
        if lead:
            groups.append(ranks([b[:head, :tok] for b in blocks]))
            blocks = [b[head:] for b in blocks]
        backs = [leave(groups[0], blocks, tail, lead)]
        yield
        if nz > 1:
            try:
                next(far)
            except StopIteration as end:
                opposite = end.value
            if lead:
                groups.append(ranks([b[:head, :tok] for b in opposite]))
                opposite = [b[head:] for b in opposite]
            backs.append(leave(groups[1], opposite, tail, lead))
            yield
        backs = [[line.done(g) for g in group] for group in backs]
        if lead:
            tallies = [jnp.concatenate([g["count"][0] for g in groups], axis=0)]
            for dx in range(1, nx):
                parts_ = [
                    b[dx - 1][0, : g["match"].shape[0]].astype(F32) for g, b in zip(groups, backs)
                ]
                tallies.append(jnp.concatenate(parts_, axis=0))
            places(tallies)
            backs = [[g[head:] for g in group] for group in backs]
        rows = jnp.concatenate(blocks + opposite, axis=0)
        part = pick(shared["own" + tail], rows)
        for dx in range(1, nx):
            back = jnp.concatenate([b[dx - 1] for b in backs], axis=0)
            part = part + pick(shared["in"][dx - 1], back)
        part = line.go(part)
        cores = [cring.gather(line, part, half)]
        if nc > 1:
            next(cores[0])
        ys = yring.gather(line, part, half)
        pieces = []
        try:
            next(ys)
            yield
            while True:
                next(ys)
                yield
        except StopIteration as end:
            by_y = end.value
        cores += [cring.gather(line, b, half) for b in by_y[1:]]
        for g in cores[1:]:
            if nc > 1:
                next(g)
        yield
        for oy, g in zip(yring.offsets(), cores):
            try:
                while True:
                    next(g)
            except StopIteration as end:
                for oc, b in zip(cring.offsets(), end.value):
                    index = yring.coordinate(y, oy) * nc + cring.coordinate(c, oc)
                    pieces.append((index * width + lo, b))
        return pieces

    parts = {}
    cuts = FETCH if width > 512 else {"x": [width], "d": [width]}
    for name, source, tail in (("x", tokens, ""), ("d", cotangent, "_w")):
        lo = 0
        for k, w in enumerate(cuts[name]):
            parts[name + str(k)] = fetch(source, lo, lo + w, tail, name + str(k) == "x0")
            lo += w
    order = ORDER.split() if (nz, nx, ny, nc) == (4, 2, 2, 2) else []
    got = run(parts, order)

    full = {}
    for name in ("x", "d"):
        whole = jnp.zeros((capacity, n_tp * width), BF)
        for k in range(len(cuts[name])):
            for column, piece in got[name + str(k)]:
                whole = lax.dynamic_update_slice(whole, piece, (0, column))
        full[name] = whole

    inputs, routed = full["x"], full["d"]
    hidden = jnp.dot(inputs, w_up, preferred_element_type=F32)
    act_full, slope = silu_parts(hidden)
    act = act_full.astype(BF)
    d_act = lax.dot_general(routed, w_down, (((1,), (1,)), ((), ())), preferred_element_type=F32)
    d_hidden = (d_act * slope).astype(BF)
    d_hidden = line.done(d_hidden)

    def give(lo, hi):
        w = hi - lo
        by_y = []
        for oy in yring.offsets():
            by_c = []
            for oc in cring.offsets():
                index = yring.coordinate(y, oy) * nc + cring.coordinate(c, oc)
                part = lax.dynamic_slice(w_up, (index * width + lo, 0), (w, hid))
                by_c.append(
                    lax.dot_general(
                        d_hidden, part, (((1,), (1,)), ((), ())), preferred_element_type=F32
                    )
                )
            by_y.append(by_c)
        stack = [jnp.concatenate([b[i] for b in by_y], axis=0) for i in range(nc)]
        summed = yield from cring.reduce(line, stack, half)
        summed = summed.reshape(ny, capacity, w)
        total = yield from yring.reduce(line, [summed[i] for i in range(ny)], half)
        total = total.astype(BF)
        backs = []
        for dx in range(1, nx):
            out = line.go(unpick(shared["in"][dx - 1], total).astype(BF))
            backs.append(cross(out, -dx))
        mine = unpick(shared["own"], total).reshape(nz, tok, w)
        if backs:
            yield
        for dx, back in enumerate(backs, 1):
            back = line.done(back).reshape(nz, slot, w)
            mine = mine + lax.dot_general(
                shared["out"][dx - 1], back, (((1,), (1,)), ((0,), (0,))), preferred_element_type=F32
            )
        result = yield from zring.reduce(line, [mine[i] for i in range(nz)], tok // 2)
        return result.astype(BF)

    parts = {"g%d" % k: give(lo, hi) for k, (lo, hi) in enumerate(edges)}
    order = BACK.split() if (nz, nx, ny, nc, len(edges)) == (4, 2, 2, 2, 2) else []
    got = run(parts, order)
    results = [got["g%d" % k] for k in range(len(edges))]
    grad_up = unpick(inputs, d_hidden).astype(BF)
    grad_down = unpick(act, routed).astype(BF)
    token_grad = jnp.concatenate(results, axis=1)
    return (token_grad, grad_up[None], grad_down[None])


def solution(mesh):
    placed = (
        P("exp", "tp"),
        P("exp", "tp"),
        P("exp", None, "tp"),
        P("exp", "tp", None),
        P("exp", None),
        P("exp", None),
    )
    return jax.shard_map(
        per_device,
        mesh=mesh,
        in_specs=placed,
        out_specs=(P("exp", "tp"), P("exp", None, "tp"), P("exp", "tp", None)),
        check_vma=False,
    )
```

```python
import functools
import math

import jax
import jax.numpy as jnp
from jax import lax
from jax.experimental import pallas as pl
from jax.experimental.pallas import tpu as pltpu
from jax.sharding import PartitionSpec as P

BF = jnp.bfloat16
F32 = jnp.float32
ORDER = [
    "x0", "x1", "x0", "x0", "x1", "x0", "d0", "x1", "x1", "x0", "d0", "d0", "d1", "x1", "d0", "x0",
    "d1", "x0", "d0", "d1", "d1", "x1", "d1", "x1", "d0", "d0", "h", "d1", "d1",
]
HEAD = 16
COST = {"leave": 300, "places": 300, "pick": 60, "slots": 300, "terms": 300}
BACK = [
    "g0", "g1", "g0", "g2", "g1", "g2", "w", "w", "u", "u", "g0", "g0", "g0", "g1", "g2", "g1",
    "g0", "g1", "g2", "g2", "g0", "g1", "g2", "g2", "g1",
]
PINS = [
    "d0A", "d1A", "g1B", "g2C",
]


def ring_order(count):
    if count <= 4:
        return list(range(0, count, 2)) + list(range(1, count, 2))[::-1]
    return list(range(count))


def lookup(table, index):
    return sum(jnp.where(index == i, jnp.int32(v), jnp.int32(0)) for i, v in enumerate(table))


class Ring:
    def __init__(self, axis, size, count, stride):
        self.axis, self.count, self.stride = axis, count, stride
        self.order = ring_order(count)
        self.half = count // 2
        spot = {c: i for i, c in enumerate(self.order)}
        self.perms = {}
        for step in (1, -1):
            pairs = []
            for index in range(size):
                c = (index // stride) % count
                there = self.order[(spot[c] + step) % count]
                pairs.append((index, index + (there - c) * stride))
            self.perms[step] = pairs
        self.spot = [spot[c] for c in range(count)]

    def send(self, value, step):
        return lax.ppermute(value, self.axis, self.perms[step])

    def coordinate(self, mine, offset):
        place = lookup(self.spot, mine)
        return lookup(self.order, lax.rem(place + offset + self.count, self.count))

    def offsets(self):
        found = [0]
        for d in range(1, self.half):
            found += [-d, d]
        return found + ([self.half] if self.count > 1 else [])

    def near(self, line, value):
        blocks = {0: value}
        up = down = value
        for d in range(1, self.half):
            up, down = self.send(up, 1), self.send(down, -1)
            yield
            up, down = line.done(up, down)
            blocks[-d], blocks[d] = up, down
        return [blocks[o] for o in self.offsets() if o in blocks]

    def far(self, line, blocks, cut):
        if self.count == 1:
            return []
        if self.count == 2:
            got = self.send(blocks[0], 1)
            yield
            return [line.done(got)]
        up, down = line.go(blocks[-2][:cut], blocks[-1][cut:])
        up, down = self.send(up, 1), self.send(down, -1)
        yield
        return list(line.done(up, down))

    def gather(self, line, value, cut):
        blocks = yield from self.near(line, value)
        far = yield from self.far(line, blocks, cut)
        return blocks + ([jnp.concatenate(far, axis=0)] if len(far) > 1 else far)

    def reduce(self, line, far, near):
        if self.count == 1:
            return near()[0]
        if self.count == 2:
            got = self.send(line.go(*far()), 1)
            yield
            return near()[0] + line.done(got).astype(F32)
        up, down = line.go(*far())
        cut = up.shape[0]
        up, down = self.send(up, 1), self.send(down, -1)
        yield
        term = near()
        for d in range(self.half - 1, 0, -1):
            up, down = line.done(up, down)
            up, down = up.astype(F32), down.astype(F32)
            up_sum, down_sum = term[d], term[-d]
            if d == self.half - 1:
                up_sum = jnp.concatenate([up_sum[:cut] + up, up_sum[cut:]], axis=0)
                down_sum = jnp.concatenate([down_sum[:cut], down_sum[cut:] + down], axis=0)
            else:
                up_sum, down_sum = up_sum + up, down_sum + down
            up, down = line.go(up_sum.astype(BF), down_sum.astype(BF))
            up, down = self.send(up, 1), self.send(down, -1)
            yield
        up, down = line.done(up, down)
        return term[0] + up.astype(F32) + down.astype(F32)

    def halves(self, term, cut):
        return [term] if self.count == 2 else [term[:cut], term[cut:]]


class Line:
    def __init__(self):
        self.mark = jnp.zeros((8, 128), F32)

    def go(self, *values):
        out = lax.optimization_barrier((*values, self.mark))
        return out[0] if len(values) == 1 else out[:-1]

    def pin(self, value, label):
        return self.done(value) if label in PINS else self.go(value)

    def done(self, *values):
        out = lax.optimization_barrier((*values, self.mark))
        self.mark = out[-1]
        return out[0] if len(values) == 1 else out[:-1]


def run(parts, order, results):
    def step(name):
        if name not in results:
            try:
                with jax.named_scope(name):
                    next(parts[name])
            except StopIteration as end:
                results[name] = end.value

    for name in order:
        step(name)
    while len(results) < len(parts):
        for name in parts:
            step(name)


def kernel_call(kind, body, outs, scalars, *arrays):
    vmem, smem = pl.BlockSpec(memory_space=pltpu.VMEM), pl.BlockSpec(memory_space=pltpu.SMEM)
    many = isinstance(outs, (list, tuple))
    return pl.pallas_call(
        body,
        out_shape=outs,
        in_specs=[smem] * len(scalars) + [vmem] * len(arrays),
        out_specs=[vmem] * len(outs) if many else vmem,
        compiler_params=pltpu.CompilerParams(vmem_limit_bytes=32 * 2**20),
        cost_estimate=pl.CostEstimate(
            flops=COST[kind] * 10**8, bytes_accessed=COST[kind] * 10**5, transcendentals=0
        ),
    )(*scalars, *arrays)


def shape(rows, columns, dtype=BF):
    return jax.ShapeDtypeStruct((rows, columns), dtype)


class Blocks:
    def __init__(self):
        self.arrays, self.parts = [], []

    def add(self, pieces, skip):
        found = []
        for k, piece in enumerate(pieces):
            lead = skip if k == 0 else 0
            found.append((len(self.arrays), lead, piece.shape[0] - lead))
            self.arrays.append(piece)
        self.parts.append(found)

    def joined(self, other):
        both = Blocks()
        both.arrays = self.arrays + other.arrays
        both.parts = self.parts + [
            [(a + len(self.arrays), r, n) for a, r, n in found] for found in other.parts
        ]
        return both


def rows_dot(onehot, refs, parts):
    total, at = 0.0, 0
    for number, first, count in parts:
        total += jnp.dot(
            onehot[:, at : at + count],
            refs[number][first : first + count, :],
            preferred_element_type=F32,
        )
        at += count
    return total


def matches(lines, expert, top):
    hit = weight = 0.0
    for k in range(top):
        same = lines[k : k + 1] == expert
        hit += jnp.where(same, 1.0, 0.0)
        weight += jnp.where(same, lines[top + k : top + k + 1], 0.0)
    return hit, weight


def stack_rows(rows, height):
    index = lax.broadcasted_iota(jnp.int32, (height, rows[0].shape[1]), 0)
    total = 0.0
    for i, row in enumerate(rows):
        total += jnp.where(index == i, jnp.broadcast_to(row, index.shape), 0.0)
    return total


def ranks_in_group(hits):
    tok = hits.shape[1]
    before = lax.broadcasted_iota(jnp.int32, (tok, tok), 0)
    after = lax.broadcasted_iota(jnp.int32, (tok, tok), 1)
    below = jnp.where(before < after, 1.0, 0.0).astype(BF)
    return jnp.dot(hits.astype(BF), below, preferred_element_type=F32)


def leave_kernel(blocks, metas, tok, top, slot, scaled, expert_ref, *refs):
    refs, out = refs[:-1], refs[-1]
    expert = expert_ref[0].astype(F32)
    found = []
    for number, first in metas:
        lines = refs[number][first : first + HEAD, :tok].astype(F32)
        found.append(matches(lines, expert, top))
    local = ranks_in_group(stack_rows([h for h, _ in found], HEAD))
    place = lax.broadcasted_iota(jnp.int32, (slot, tok), 0).astype(F32)
    for i, parts in enumerate(blocks.parts):
        hit, weight = found[i]
        rank = jnp.where(hit > 0.0, local[i : i + 1], -1.0)
        value = weight if scaled else hit
        onehot = jnp.where(place == rank, value, 0.0).astype(BF)
        out[i * slot : (i + 1) * slot, :] = rows_dot(onehot, refs, parts).astype(BF)


def places_kernel(spots, tok, top, slot, own, nx, *refs):
    experts, earlier_ref = refs[:nx], refs[nx]
    refs, (rank_ref, weight_ref, in_ref, out_ref) = refs[nx + 1 : -4], refs[-4:]
    expert = experts[0][0].astype(F32)
    height = earlier_ref.shape[0]
    found = []
    for number, first in spots:
        lines = refs[number][first : first + 2 * top, :tok].astype(F32)
        found.append(matches(lines, expert, top))
    hits = stack_rows([h for h, _ in found], height)
    local = ranks_in_group(hits)
    count = jnp.broadcast_to(jnp.sum(hits, axis=1, keepdims=True), (height, 128))
    base = jnp.dot(earlier_ref[...], count.astype(BF), preferred_element_type=F32)
    lane = lax.broadcasted_iota(jnp.int32, (1, slot), 1).astype(F32)
    for i, (hit, weight) in enumerate(found):
        start = base[i : i + 1, :1]
        if i < own:
            rank_ref[i : i + 1, :] = jnp.where(hit > 0.0, local[i : i + 1] + start, -1.0)
            weight_ref[i : i + 1, :] = weight
        else:
            there = jnp.where(lane < count[i : i + 1, :1], start + lane, -1.0)
            in_ref[i - own : i - own + 1, :] = there
    for dx in range(1, nx):
        rows = []
        for number, first in spots[:own]:
            lines = refs[number][first : first + 2 * top, :tok].astype(F32)
            rows.append(matches(lines, experts[dx][0].astype(F32), top)[0])
        hits = stack_rows(rows, height)
        local = jnp.where(hits > 0.0, ranks_in_group(hits), -1.0)
        out_ref[(dx - 1) * own : dx * own, :] = local[:own]


def pick_kernel(blocks, backs, tok, slot, tile, scaled, rank_ref, weight_ref, in_ref, *refs):
    refs, out = refs[:-1], refs[-1]

    def step(number, carry):
        first = pl.multiple_of(number * tile, tile)

        def onehot(ranks, value, columns):
            place = lax.broadcasted_iota(jnp.int32, (tile, columns), 0) + first
            return jnp.where(place.astype(F32) == ranks, value, 0.0).astype(BF)

        total = 0.0
        for i, parts in enumerate(blocks.parts):
            value = weight_ref[i : i + 1, :] if scaled else 1.0
            total += rows_dot(onehot(rank_ref[i : i + 1, :], value, tok), refs, parts)
        for i, parts in enumerate(backs.parts):
            total += rows_dot(onehot(in_ref[i : i + 1, :], 1.0, slot), refs, parts)
        out[pl.ds(first, tile), :] = total.astype(BF)
        return carry

    lax.fori_loop(0, out.shape[0] // tile, step, 0)


def chosen(ranks, height):
    place = lax.broadcasted_iota(jnp.int32, (height, ranks.shape[1]), 0).astype(F32)
    return jnp.where(place == ranks, 1.0, 0.0).astype(BF)


def turned_dot(onehot, rows):
    return lax.dot_general(onehot, rows, (((0,), (0,)), ((), ())), preferred_element_type=F32)


def slots_kernel(first, slot, in_ref, total_ref, out_ref):
    total = total_ref[...]
    for i in range(out_ref.shape[0] // slot):
        onehot = chosen(in_ref[first + i : first + i + 1, :], total.shape[0])
        out_ref[i * slot : (i + 1) * slot, :] = turned_dot(onehot, total).astype(BF)


def terms_kernel(first, nz, slot, backs, rank_ref, slots_ref, total_ref, *refs):
    back_refs, outs = refs[:backs], refs[backs:]
    total = total_ref[...]
    for i, out in enumerate(outs):
        sum_ = turned_dot(chosen(rank_ref[first + i : first + i + 1, :], total.shape[0]), total)
        for k, back in enumerate(back_refs):
            line = k * nz + first + i
            rows = back[i * slot : (i + 1) * slot, :]
            sum_ += turned_dot(chosen(slots_ref[line : line + 1, :], slot), rows)
        out[...] = sum_.astype(out.dtype)


def unpick(onehot, rows):
    return lax.dot_general(onehot, rows, (((0,), (0,)), ((), ())), preferred_element_type=F32)


def silu_parts(hidden):
    sigma = jax.nn.sigmoid(hidden)
    return (hidden * sigma, sigma * (1.0 + hidden * (1.0 - sigma)))


def per_device(tokens, cotangent, up_weight, down_weight, expert_ids, gate_probs):
    tok, top = expert_ids.shape
    width = tokens.shape[1]
    n_exp, n_tp = lax.axis_size("exp"), lax.axis_size("tp")
    experts = n_exp * up_weight.shape[0]
    slot = min(4 * tok // experts, tok)
    capacity = 5 * tok * n_exp // (2 * experts)
    nx = 2 ** (int(math.log2(n_exp)) // 2)
    nz = n_exp // nx
    nc = 2 if n_tp % 2 == 0 else 1
    ny = n_tp // nc
    zring, yring, cring = (
        Ring("exp", n_exp, nz, nx),
        Ring("tp", n_tp, ny, nc),
        Ring("tp", n_tp, nc, 1),
    )
    e, t = lax.axis_index("exp"), lax.axis_index("tp")
    z, x, y, c = lax.div(e, nx), lax.rem(e, nx), lax.div(t, nc), lax.rem(t, nc)

    def cross(value, dx):
        pairs = [(i, i // nx * nx + (i % nx + dx) % nx) for i in range(n_exp)]
        return lax.ppermute(value, "exp", pairs)

    w_up, w_down = up_weight[0], down_weight[0]
    hid = w_up.shape[1]

    lanes = width // 128
    if width % 128 == 0 and lanes >= 4:
        small = lanes * 3 // 7 * 128
        cuts = {"x": [width - small, small], "d": [width - small, small]}
    else:
        cuts = {"x": [width], "d": [width]}

    meta = jnp.concatenate([expert_ids.astype(BF).T, gate_probs.T], axis=0)
    lines = 2 * top
    swaps = [cross(meta, dx) for dx in range(1, nx)]

    def headed(rows, piece):
        rows = jnp.pad(rows, ((0, HEAD - rows.shape[0]), (0, piece.shape[1] - tok)))
        return jnp.concatenate([rows, piece], axis=0)

    line = Line()
    shared = {}
    half = capacity // 2
    tile = math.gcd(capacity, 128)
    zs = [zring.coordinate(z, o) for o in zring.offsets()]
    columns = [lax.rem(x - dx + nx, nx) for dx in range(nx)]
    number = jnp.stack([zc * nx + xc for xc in columns for zc in zs])
    high = -(-n_exp // 16) * 16
    earlier = (number[None, :] < number[:, None]).astype(BF)
    earlier = jnp.pad(earlier, ((0, high - n_exp), (0, high - n_exp)))
    me = jnp.reshape(e, (1,)).astype(jnp.int32)
    over = [jnp.reshape(z * nx + lax.rem(x + dx, nx), (1,)).astype(jnp.int32) for dx in range(1, nx)]

    def leave(blocks, metas, scaled, label):
        arrays = blocks.arrays + [m for m, _ in metas]
        spots = [(len(blocks.arrays) + k, first) for k, (_, first) in enumerate(metas)]
        backs = []
        for dx in range(1, nx):
            body = functools.partial(leave_kernel, blocks, spots, tok, top, slot, scaled)
            out = shape(len(blocks.parts) * slot, blocks.arrays[0].shape[1])
            sent = kernel_call("leave", body, out, [over[dx - 1]], *arrays)
            backs.append(cross(line.pin(sent, label), dx))
        return backs

    def places():
        arrays = shared["own"] + shared["others"]
        spots = [(i, 0) for i in range(nz)]
        for dx in range(1, nx):
            spots += [(nz + i, (dx - 1) * lines) for i in range(nz)]
        body = functools.partial(places_kernel, spots, tok, top, slot, nz, nx)
        many = max(1, nx - 1) * nz
        outs = [shape(nz, tok, F32), shape(nz, tok, F32), shape(many, slot, F32), shape(many, tok, F32)]
        *shared["places"], shared["slots"] = kernel_call("places", body, outs, [me] + over, earlier, *arrays)

    def fetch(source, lo, hi, scaled, number, label):
        skip = HEAD if number < 2 else 0
        piece = source[:, lo:hi]
        if number == 0:
            piece = headed(meta, piece)
        if number == 1:
            others = [line.done(g) for g in swaps]
            piece = headed(jnp.concatenate(others, axis=0) if others else meta, piece)
        piece = line.go(piece)
        near = yield from zring.near(line, piece)
        far = zring.far(line, near, skip + tok // 2)
        opposite = []
        try:
            next(far)
        except StopIteration as end:
            opposite = end.value
        yield
        blocks = Blocks()
        for b in near:
            blocks.add([b], skip)
        if number == 0:
            shared["own"] = list(near)
        if number == 1:
            shared["others"] = list(near)
        metas = [(m, 0) for m in shared["own"][: len(near)]]
        backs = [leave(blocks, metas, scaled, label + "A")]
        yield
        if nz > 1:
            try:
                next(far)
            except StopIteration as end:
                opposite = end.value
            if number == 0:
                shared["own"].append(opposite[0])
            if number == 1:
                shared["others"].append(opposite[0])
            last = Blocks()
            last.add(opposite, skip)
            backs.append(leave(last, [(shared["own"][-1], 0)], scaled, label + "B"))
            blocks = blocks.joined(last)
            yield
        backs = [[line.done(g) for g in group] for group in backs]
        if "places" not in shared:
            places()
        arrived = Blocks()
        for dx in range(1, nx):
            for group in backs:
                at = len(arrived.arrays)
                arrived.arrays.append(group[dx - 1])
                for r in range(0, group[dx - 1].shape[0], slot):
                    arrived.parts.append([(at, r, slot)])
        shifted = blocks.joined(arrived)
        arrived.parts = shifted.parts[len(blocks.parts) :]
        body = functools.partial(pick_kernel, blocks, arrived, tok, slot, tile, scaled)
        part = kernel_call("pick", body, shape(capacity, hi - lo), [], *shared["places"], *shifted.arrays)
        part = line.pin(part, label + "P")
        cores = [cring.gather(line, part, half)]
        if nc > 1:
            next(cores[0])
        ys = yring.gather(line, part, half)
        pieces = []
        try:
            next(ys)
            yield
            while True:
                next(ys)
                yield
        except StopIteration as end:
            by_y = end.value
        cores += [cring.gather(line, b, half) for b in by_y[1:]]
        for g in cores[1:]:
            if nc > 1:
                next(g)
        yield
        for oy, g in zip(yring.offsets(), cores):
            try:
                while True:
                    next(g)
            except StopIteration as end:
                for oc, b in zip(cring.offsets(), end.value):
                    index = yring.coordinate(y, oy) * nc + cring.coordinate(c, oc)
                    pieces.append((index * width + lo, b))
        return pieces

    parts = {}
    for name, source in (("x", tokens), ("d", cotangent)):
        lo = 0
        for k, w in enumerate(cuts[name]):
            parts[name + str(k)] = fetch(
                source, lo, lo + w, name == "d", len(parts), name + str(k)
            )
            lo += w
    def assembled(names):
        whole = jnp.zeros((capacity, n_tp * width), BF)
        for name in names:
            for column, piece in done[name]:
                whole = lax.dynamic_update_slice(whole, piece, (0, column))
        return whole

    def first_half():
        names = [name for name in parts if name[0] == "x"]
        while any(name not in done for name in names):
            yield
        inputs = assembled(names)
        hidden = jnp.dot(inputs, w_up, preferred_element_type=F32)
        return inputs, line.done(hidden)

    done = {}
    parts["h"] = first_half()
    order = ORDER if (nz, nx, ny, nc, len(parts)) == (4, 2, 2, 2, 5) else []
    run(parts, order, done)

    inputs, hidden = done["h"]
    routed = assembled([name for name in parts if name[0] == "d"])
    act_full, slope = silu_parts(hidden)
    act = act_full.astype(BF)
    d_act = lax.dot_general(routed, w_down, (((1,), (1,)), ((), ())), preferred_element_type=F32)
    d_hidden = (d_act * slope).astype(BF)
    d_hidden = line.done(d_hidden)

    rank, weight, there = shared["places"]
    taken = shared["slots"]

    def give(lo, hi, label):
        w = hi - lo

        def term(oy, oc):
            index = yring.coordinate(y, oy) * nc + cring.coordinate(c, oc)
            part = lax.dynamic_slice(w_up, (index * width + lo, 0), (w, hid))
            return lax.dot_general(
                line.go(d_hidden), part, (((1,), (1,)), ((), ())), preferred_element_type=F32
            )

        def of_core(oc):
            return jnp.concatenate([term(oy, oc) for oy in yring.offsets()], axis=0)

        if nc > 1:
            other = cring.send(line.pin(of_core(1).astype(BF), label + "C"), 1)
            yield
            summed = of_core(0) + line.done(other).astype(F32)
        else:
            summed = of_core(0)
        summed = summed.reshape(ny, capacity, w)
        by_y = dict(zip(yring.offsets(), [summed[i] for i in range(ny)]))
        total = yield from yring.reduce(
            line, lambda: [p.astype(BF) for p in yring.halves(by_y[yring.half], half)], lambda: by_y
        )
        total = total.astype(BF)

        def across(first, groups):
            backs = []
            for dx in range(1, nx):
                body = functools.partial(slots_kernel, (dx - 1) * nz + first, slot)
                out = kernel_call("slots", body, shape(groups * slot, w), [], there, total)
                backs.append(cross(line.pin(out, label + "AB"[first > 0]), -dx))
            return backs

        def terms(first, groups, backs, kind):
            backs = [line.done(b) for b in backs]
            body = functools.partial(terms_kernel, first, nz, slot, len(backs))
            outs = [shape(tok, w, kind)] * groups
            return kernel_call("terms", body, outs, [], rank, taken, total, *backs)

        far_backs = across(nz - 1, 1) if nz > 1 else []
        if far_backs:
            yield
        near_backs = across(0, max(1, nz - 1))
        if near_backs:
            yield

        def far():
            return zring.halves(terms(nz - 1, 1, far_backs, BF)[0], tok // 2)

        def near():
            found = terms(0, max(1, nz - 1), near_backs, F32)
            return dict(zip(zring.offsets(), found))

        result = yield from zring.reduce(line, far, near)
        return result.astype(BF)

    if width % 128 == 0 and lanes >= 6:
        third = lanes // 3 * 128
        back_cuts = [width - 2 * third, third, third]
    else:
        back_cuts = [width]
    parts, lo = {}, 0
    for k, w in enumerate(back_cuts):
        parts["g%d" % k] = give(lo, lo + w, "g%d" % k)
        lo += w
    def weights(left, right):
        yield
        return line.done(unpick(line.go(left), right).astype(BF))

    parts["u"], parts["w"] = weights(d_hidden, inputs), weights(act, routed)
    order = BACK if (nz, nx, ny, nc, len(parts)) == (4, 2, 2, 2, 5) else []
    got = {}
    run(parts, order, got)
    results = [got["g%d" % k] for k in range(len(back_cuts))]
    grad_up, grad_down = got["u"].T, got["w"]
    token_grad = jnp.concatenate(results, axis=1)
    return (token_grad, grad_up[None], grad_down[None])


def solution(mesh):
    placed = (
        P("exp", "tp"),
        P("exp", "tp"),
        P("exp", None, "tp"),
        P("exp", "tp", None),
        P("exp", None),
        P("exp", None),
    )
    return jax.shard_map(
        per_device,
        mesh=mesh,
        in_specs=placed,
        out_specs=(P("exp", "tp"), P("exp", None, "tp"), P("exp", "tp", None)),
        check_vma=False,
    )
```

```python
import functools
import math

import jax
import jax.numpy as jnp
from jax import lax
from jax.experimental import pallas as pl
from jax.experimental.pallas import tpu as pltpu
from jax.sharding import PartitionSpec as P

BF = jnp.bfloat16
F32 = jnp.float32
ORDER = [
    "x0", "x1", "x0", "x0", "x1", "x0", "d0", "x1", "x1", "x0", "d0", "d0", "d1", "x1", "d0", "x0",
    "d1", "x0", "d0", "d1", "d1", "x1", "d1", "x1", "d0", "d0", "h", "d1", "d1",
]
HEAD = 16
COST = {"leave": 300, "places": 300, "pick": 60, "slots": 300, "terms": 300}
BACK = [
    "g0", "g1", "g0", "g2", "g1", "g2", "w", "w", "u", "u", "g0", "g0", "g0", "g1", "g2", "g1",
    "g0", "g1", "g2", "g2", "g0", "g1", "g2", "g2", "g1",
]
PINS = [
    "d0A", "d1A", "g1B", "g2C",
]


def ring_order(count):
    if count <= 4:
        return list(range(0, count, 2)) + list(range(1, count, 2))[::-1]
    return list(range(count))


def lookup(table, index):
    return sum(jnp.where(index == i, jnp.int32(v), jnp.int32(0)) for i, v in enumerate(table))


class Ring:
    def __init__(self, axis, size, count, stride):
        self.axis, self.count, self.stride = axis, count, stride
        self.order = ring_order(count)
        self.half = count // 2
        spot = {c: i for i, c in enumerate(self.order)}
        self.perms = {}
        for step in (1, -1):
            pairs = []
            for index in range(size):
                c = (index // stride) % count
                there = self.order[(spot[c] + step) % count]
                pairs.append((index, index + (there - c) * stride))
            self.perms[step] = pairs
        self.spot = [spot[c] for c in range(count)]

    def send(self, value, step):
        return lax.ppermute(value, self.axis, self.perms[step])

    def coordinate(self, mine, offset):
        place = lookup(self.spot, mine)
        return lookup(self.order, lax.rem(place + offset + self.count, self.count))

    def offsets(self):
        found = [0]
        for d in range(1, self.half):
            found += [-d, d]
        return found + ([self.half] if self.count > 1 else [])

    def near(self, line, value):
        blocks = {0: value}
        up = down = value
        for d in range(1, self.half):
            up, down = self.send(up, 1), self.send(down, -1)
            yield
            up, down = line.done(up, down)
            blocks[-d], blocks[d] = up, down
        return [blocks[o] for o in self.offsets() if o in blocks]

    def far(self, line, blocks, cut):
        if self.count == 1:
            return []
        if self.count == 2:
            got = self.send(blocks[0], 1)
            yield
            return [line.done(got)]
        up, down = line.go(blocks[-2][:cut], blocks[-1][cut:])
        up, down = self.send(up, 1), self.send(down, -1)
        yield
        return list(line.done(up, down))

    def gather(self, line, value, cut):
        blocks = yield from self.near(line, value)
        far = yield from self.far(line, blocks, cut)
        return blocks + ([jnp.concatenate(far, axis=0)] if len(far) > 1 else far)

    def reduce(self, line, far, near):
        if self.count == 1:
            return near()[0]
        if self.count == 2:
            got = self.send(line.go(*far()), 1)
            yield
            return near()[0] + line.done(got).astype(F32)
        up, down = line.go(*far())
        cut = up.shape[0]
        up, down = self.send(up, 1), self.send(down, -1)
        yield
        term = near()
        for d in range(self.half - 1, 0, -1):
            up, down = line.done(up, down)
            up, down = up.astype(F32), down.astype(F32)
            up_sum, down_sum = term[d], term[-d]
            if d == self.half - 1:
                up_sum = jnp.concatenate([up_sum[:cut] + up, up_sum[cut:]], axis=0)
                down_sum = jnp.concatenate([down_sum[:cut], down_sum[cut:] + down], axis=0)
            else:
                up_sum, down_sum = up_sum + up, down_sum + down
            up, down = line.go(up_sum.astype(BF), down_sum.astype(BF))
            up, down = self.send(up, 1), self.send(down, -1)
            yield
        up, down = line.done(up, down)
        return term[0] + up.astype(F32) + down.astype(F32)

    def halves(self, term, cut):
        return [term] if self.count == 2 else [term[:cut], term[cut:]]


class Line:
    def __init__(self):
        self.mark = jnp.zeros((8, 128), F32)

    def go(self, *values):
        out = lax.optimization_barrier((*values, self.mark))
        return out[0] if len(values) == 1 else out[:-1]

    def pin(self, value, label):
        return self.done(value) if label in PINS else self.go(value)

    def done(self, *values):
        out = lax.optimization_barrier((*values, self.mark))
        self.mark = out[-1]
        return out[0] if len(values) == 1 else out[:-1]


def run(parts, order, results):
    def step(name):
        if name not in results:
            try:
                with jax.named_scope(name):
                    next(parts[name])
            except StopIteration as end:
                results[name] = end.value

    for name in order:
        step(name)
    while len(results) < len(parts):
        for name in parts:
            step(name)


def kernel_call(kind, body, outs, scalars, *arrays):
    vmem, smem = pl.BlockSpec(memory_space=pltpu.VMEM), pl.BlockSpec(memory_space=pltpu.SMEM)
    many = isinstance(outs, (list, tuple))
    return pl.pallas_call(
        body,
        out_shape=outs,
        in_specs=[smem] * len(scalars) + [vmem] * len(arrays),
        out_specs=[vmem] * len(outs) if many else vmem,
        compiler_params=pltpu.CompilerParams(vmem_limit_bytes=32 * 2**20),
        cost_estimate=pl.CostEstimate(
            flops=COST[kind] * 10**8, bytes_accessed=COST[kind] * 10**5, transcendentals=0
        ),
    )(*scalars, *arrays)


def shape(rows, columns, dtype=BF):
    return jax.ShapeDtypeStruct((rows, columns), dtype)


class Blocks:
    def __init__(self):
        self.arrays, self.parts = [], []

    def add(self, pieces, skip):
        found = []
        for k, piece in enumerate(pieces):
            lead = skip if k == 0 else 0
            found.append((len(self.arrays), lead, piece.shape[0] - lead))
            self.arrays.append(piece)
        self.parts.append(found)

    def joined(self, other):
        both = Blocks()
        both.arrays = self.arrays + other.arrays
        both.parts = self.parts + [
            [(a + len(self.arrays), r, n) for a, r, n in found] for found in other.parts
        ]
        return both


def rows_dot(onehot, refs, parts):
    total, at = 0.0, 0
    for number, first, count in parts:
        total += jnp.dot(
            onehot[:, at : at + count],
            refs[number][first : first + count, :],
            preferred_element_type=F32,
        )
        at += count
    return total


def matches(lines, expert, top):
    hit = weight = 0.0
    for k in range(top):
        same = lines[k : k + 1] == expert
        hit += jnp.where(same, 1.0, 0.0)
        weight += jnp.where(same, lines[top + k : top + k + 1], 0.0)
    return hit, weight


def stack_rows(rows, height):
    index = lax.broadcasted_iota(jnp.int32, (height, rows[0].shape[1]), 0)
    total = 0.0
    for i, row in enumerate(rows):
        total += jnp.where(index == i, jnp.broadcast_to(row, index.shape), 0.0)
    return total


def ranks_in_group(hits):
    tok = hits.shape[1]
    before = lax.broadcasted_iota(jnp.int32, (tok, tok), 0)
    after = lax.broadcasted_iota(jnp.int32, (tok, tok), 1)
    below = jnp.where(before < after, 1.0, 0.0).astype(BF)
    return jnp.dot(hits.astype(BF), below, preferred_element_type=F32)


def leave_kernel(blocks, metas, tok, top, slot, scaled, expert_ref, *refs):
    refs, out = refs[:-1], refs[-1]
    expert = expert_ref[0].astype(F32)
    found = []
    for number, first in metas:
        lines = refs[number][first : first + HEAD, :tok].astype(F32)
        found.append(matches(lines, expert, top))
    local = ranks_in_group(stack_rows([h for h, _ in found], HEAD))
    place = lax.broadcasted_iota(jnp.int32, (slot, tok), 0).astype(F32)
    for i, parts in enumerate(blocks.parts):
        hit, weight = found[i]
        rank = jnp.where(hit > 0.0, local[i : i + 1], -1.0)
        value = weight if scaled else hit
        onehot = jnp.where(place == rank, value, 0.0).astype(BF)
        out[i * slot : (i + 1) * slot, :] = rows_dot(onehot, refs, parts).astype(BF)


def places_kernel(spots, tok, top, slot, own, nx, *refs):
    experts, earlier_ref = refs[:nx], refs[nx]
    refs, (rank_ref, weight_ref, in_ref, out_ref) = refs[nx + 1 : -4], refs[-4:]
    expert = experts[0][0].astype(F32)
    height = earlier_ref.shape[0]
    found = []
    for number, first in spots:
        lines = refs[number][first : first + 2 * top, :tok].astype(F32)
        found.append(matches(lines, expert, top))
    hits = stack_rows([h for h, _ in found], height)
    local = ranks_in_group(hits)
    count = jnp.broadcast_to(jnp.sum(hits, axis=1, keepdims=True), (height, 128))
    base = jnp.dot(earlier_ref[...], count.astype(BF), preferred_element_type=F32)
    lane = lax.broadcasted_iota(jnp.int32, (1, slot), 1).astype(F32)
    for i, (hit, weight) in enumerate(found):
        start = base[i : i + 1, :1]
        if i < own:
            rank_ref[i : i + 1, :] = jnp.where(hit > 0.0, local[i : i + 1] + start, -1.0)
            weight_ref[i : i + 1, :] = weight
        else:
            there = jnp.where(lane < count[i : i + 1, :1], start + lane, -1.0)
            in_ref[i - own : i - own + 1, :] = there
    for dx in range(1, nx):
        rows = []
        for number, first in spots[:own]:
            lines = refs[number][first : first + 2 * top, :tok].astype(F32)
            rows.append(matches(lines, experts[dx][0].astype(F32), top)[0])
        hits = stack_rows(rows, height)
        local = jnp.where(hits > 0.0, ranks_in_group(hits), -1.0)
        out_ref[(dx - 1) * own : dx * own, :] = local[:own]


def pick_kernel(blocks, backs, tok, slot, tile, scaled, rank_ref, weight_ref, in_ref, *refs):
    refs, out = refs[:-1], refs[-1]

    def step(number, carry):
        first = pl.multiple_of(number * tile, tile)

        def onehot(ranks, value, columns):
            place = lax.broadcasted_iota(jnp.int32, (tile, columns), 0) + first
            return jnp.where(place.astype(F32) == ranks, value, 0.0).astype(BF)

        total = 0.0
        for i, parts in enumerate(blocks.parts):
            value = weight_ref[i : i + 1, :] if scaled else 1.0
            total += rows_dot(onehot(rank_ref[i : i + 1, :], value, tok), refs, parts)
        for i, parts in enumerate(backs.parts):
            total += rows_dot(onehot(in_ref[i : i + 1, :], 1.0, slot), refs, parts)
        out[pl.ds(first, tile), :] = total.astype(BF)
        return carry

    lax.fori_loop(0, out.shape[0] // tile, step, 0)


def chosen(ranks, height):
    place = lax.broadcasted_iota(jnp.int32, (height, ranks.shape[1]), 0).astype(F32)
    return jnp.where(place == ranks, 1.0, 0.0).astype(BF)


def turned_dot(onehot, rows):
    return lax.dot_general(onehot, rows, (((0,), (0,)), ((), ())), preferred_element_type=F32)


def slots_kernel(first, slot, in_ref, total_ref, out_ref):
    total = total_ref[...]
    for i in range(out_ref.shape[0] // slot):
        onehot = chosen(in_ref[first + i : first + i + 1, :], total.shape[0])
        out_ref[i * slot : (i + 1) * slot, :] = turned_dot(onehot, total).astype(BF)


def terms_kernel(first, nz, slot, backs, rank_ref, slots_ref, total_ref, *refs):
    back_refs, outs = refs[:backs], refs[backs:]
    total = total_ref[...]
    for i, out in enumerate(outs):
        sum_ = turned_dot(chosen(rank_ref[first + i : first + i + 1, :], total.shape[0]), total)
        for k, back in enumerate(back_refs):
            line = k * nz + first + i
            rows = back[i * slot : (i + 1) * slot, :]
            sum_ += turned_dot(chosen(slots_ref[line : line + 1, :], slot), rows)
        out[...] = sum_.astype(out.dtype)


def unpick(onehot, rows):
    return lax.dot_general(onehot, rows, (((0,), (0,)), ((), ())), preferred_element_type=F32)


def silu_parts(hidden):
    sigma = jax.nn.sigmoid(hidden)
    return (hidden * sigma, sigma * (1.0 + hidden * (1.0 - sigma)))


def per_device(tokens, cotangent, up_weight, down_weight, expert_ids, gate_probs):
    tok, top = expert_ids.shape
    width = tokens.shape[1]
    n_exp, n_tp = lax.axis_size("exp"), lax.axis_size("tp")
    experts = n_exp * up_weight.shape[0]
    slot = min(4 * tok // experts, tok)
    capacity = 5 * tok * n_exp // (2 * experts)
    nx = 2 ** (int(math.log2(n_exp)) // 2)
    nz = n_exp // nx
    nc = 2 if n_tp % 2 == 0 else 1
    ny = n_tp // nc
    zring, yring, cring = (
        Ring("exp", n_exp, nz, nx),
        Ring("tp", n_tp, ny, nc),
        Ring("tp", n_tp, nc, 1),
    )
    e, t = lax.axis_index("exp"), lax.axis_index("tp")
    z, x, y, c = lax.div(e, nx), lax.rem(e, nx), lax.div(t, nc), lax.rem(t, nc)

    def cross(value, dx):
        pairs = [(i, i // nx * nx + (i % nx + dx) % nx) for i in range(n_exp)]
        return lax.ppermute(value, "exp", pairs)

    w_up, w_down = up_weight[0], down_weight[0]
    hid = w_up.shape[1]

    lanes = width // 128
    if width % 128 == 0 and lanes >= 4:
        small = lanes * 3 // 7 * 128
        cuts = {"x": [width - small, small], "d": [width - small, small]}
    else:
        cuts = {"x": [width], "d": [width]}

    meta = jnp.concatenate([expert_ids.T.astype(BF), gate_probs.T, jnp.zeros((HEAD - 2 * top, tok), BF)], axis=0)
    lines = 2 * top
    swaps = [cross(meta[: 2 * top], dx) for dx in range(1, nx)]

    def headed(rows, piece):
        rows = jnp.pad(rows, ((0, HEAD - rows.shape[0]), (0, piece.shape[1] - tok)))
        return jnp.concatenate([rows, piece], axis=0)

    line = Line()
    shared = {}
    half = capacity // 2
    tile = math.gcd(capacity, 128)
    zs = [zring.coordinate(z, o) for o in zring.offsets()]
    columns = [lax.rem(x - dx + nx, nx) for dx in range(nx)]
    number = jnp.stack([zc * nx + xc for xc in columns for zc in zs])
    high = -(-n_exp // 16) * 16
    earlier = (number[None, :] < number[:, None]).astype(BF)
    earlier = jnp.pad(earlier, ((0, high - n_exp), (0, high - n_exp)))
    me = jnp.reshape(e, (1,)).astype(jnp.int32)
    over = [jnp.reshape(z * nx + lax.rem(x + dx, nx), (1,)).astype(jnp.int32) for dx in range(1, nx)]

    def leave(blocks, metas, scaled, label):
        arrays = blocks.arrays + [m for m, _ in metas]
        spots = [(len(blocks.arrays) + k, first) for k, (_, first) in enumerate(metas)]
        backs = []
        for dx in range(1, nx):
            body = functools.partial(leave_kernel, blocks, spots, tok, top, slot, scaled)
            out = shape(len(blocks.parts) * slot, blocks.arrays[0].shape[1])
            sent = kernel_call("leave", body, out, [over[dx - 1]], *arrays)
            backs.append(cross(line.pin(sent, label), dx))
        return backs

    def places():
        arrays = shared["own"] + shared["others"]
        spots = [(i, 0) for i in range(nz)]
        for dx in range(1, nx):
            spots += [(nz + i, (dx - 1) * lines) for i in range(nz)]
        body = functools.partial(places_kernel, spots, tok, top, slot, nz, nx)
        many = max(1, nx - 1) * nz
        outs = [shape(nz, tok, F32), shape(nz, tok, F32), shape(many, slot, F32), shape(many, tok, F32)]
        *shared["places"], shared["slots"] = kernel_call("places", body, outs, [me] + over, earlier, *arrays)

    def fetch(source, lo, hi, scaled, number, label):
        skip = HEAD if number < 2 else 0
        piece = source[:, lo:hi]
        if number == 0:
            piece = headed(meta, piece)
        if number == 1:
            others = [line.done(g) for g in swaps]
            piece = headed(jnp.concatenate(others, axis=0) if others else meta, piece)
        piece = line.go(piece)
        near = yield from zring.near(line, piece)
        far = zring.far(line, near, skip + tok // 2)
        opposite = []
        try:
            next(far)
        except StopIteration as end:
            opposite = end.value
        yield
        blocks = Blocks()
        for b in near:
            blocks.add([b], skip)
        if number == 0:
            shared["own"] = list(near)
        if number == 1:
            shared["others"] = list(near)
        metas = [(m, 0) for m in shared["own"][: len(near)]]
        backs = [leave(blocks, metas, scaled, label + "A")]
        yield
        if nz > 1:
            try:
                next(far)
            except StopIteration as end:
                opposite = end.value
            if number == 0:
                shared["own"].append(opposite[0])
            if number == 1:
                shared["others"].append(opposite[0])
            last = Blocks()
            last.add(opposite, skip)
            backs.append(leave(last, [(shared["own"][-1], 0)], scaled, label + "B"))
            blocks = blocks.joined(last)
            yield
        backs = [[line.done(g) for g in group] for group in backs]
        if "places" not in shared:
            places()
        arrived = Blocks()
        for dx in range(1, nx):
            for group in backs:
                at = len(arrived.arrays)
                arrived.arrays.append(group[dx - 1])
                for r in range(0, group[dx - 1].shape[0], slot):
                    arrived.parts.append([(at, r, slot)])
        shifted = blocks.joined(arrived)
        arrived.parts = shifted.parts[len(blocks.parts) :]
        body = functools.partial(pick_kernel, blocks, arrived, tok, slot, tile, scaled)
        part = kernel_call("pick", body, shape(capacity, hi - lo), [], *shared["places"], *shifted.arrays)
        part = line.pin(part, label + "P")
        cores = [cring.gather(line, part, half)]
        if nc > 1:
            next(cores[0])
        ys = yring.gather(line, part, half)
        pieces = []
        try:
            next(ys)
            yield
            while True:
                next(ys)
                yield
        except StopIteration as end:
            by_y = end.value
        cores += [cring.gather(line, b, half) for b in by_y[1:]]
        for g in cores[1:]:
            if nc > 1:
                next(g)
        yield
        for oy, g in zip(yring.offsets(), cores):
            try:
                while True:
                    next(g)
            except StopIteration as end:
                for oc, b in zip(cring.offsets(), end.value):
                    index = yring.coordinate(y, oy) * nc + cring.coordinate(c, oc)
                    pieces.append((index * width + lo, b))
        return pieces

    parts = {}
    for name, source in (("x", tokens), ("d", cotangent)):
        lo = 0
        for k, w in enumerate(cuts[name]):
            parts[name + str(k)] = fetch(
                source, lo, lo + w, name == "d", len(parts), name + str(k)
            )
            lo += w
    def assembled(names):
        whole = jnp.zeros((capacity, n_tp * width), BF)
        for name in names:
            for column, piece in done[name]:
                whole = lax.dynamic_update_slice(whole, piece, (0, column))
        return whole

    def first_half():
        names = [name for name in parts if name[0] == "x"]
        while any(name not in done for name in names):
            yield
        inputs = assembled(names)
        hidden = jnp.dot(inputs, w_up, preferred_element_type=F32)
        return inputs, line.done(hidden)

    done = {}
    parts["h"] = first_half()
    order = ORDER if (nz, nx, ny, nc, len(parts)) == (4, 2, 2, 2, 5) else []
    run(parts, order, done)

    inputs, hidden = done["h"]
    routed = assembled([name for name in parts if name[0] == "d"])
    act_full, slope = silu_parts(hidden)
    act = act_full.astype(BF)
    d_act = lax.dot_general(routed, w_down, (((1,), (1,)), ((), ())), preferred_element_type=F32)
    d_hidden = (d_act * slope).astype(BF)
    d_hidden = line.done(d_hidden)

    rank, weight, there = shared["places"]
    taken = shared["slots"]

    def give(lo, hi, label):
        w = hi - lo

        def term(oy, oc):
            index = yring.coordinate(y, oy) * nc + cring.coordinate(c, oc)
            part = lax.dynamic_slice(w_up, (index * width + lo, 0), (w, hid))
            return lax.dot_general(
                line.go(d_hidden), part, (((1,), (1,)), ((), ())), preferred_element_type=F32
            )

        def of_core(oc):
            return jnp.concatenate([term(oy, oc) for oy in yring.offsets()], axis=0)

        if nc > 1:
            other = cring.send(line.pin(of_core(1).astype(BF), label + "C"), 1)
            yield
            summed = of_core(0) + line.done(other).astype(F32)
        else:
            summed = of_core(0)
        summed = summed.reshape(ny, capacity, w)
        by_y = dict(zip(yring.offsets(), [summed[i] for i in range(ny)]))
        total = yield from yring.reduce(
            line, lambda: [p.astype(BF) for p in yring.halves(by_y[yring.half], half)], lambda: by_y
        )
        total = total.astype(BF)

        def across(first, groups):
            backs = []
            for dx in range(1, nx):
                body = functools.partial(slots_kernel, (dx - 1) * nz + first, slot)
                out = kernel_call("slots", body, shape(groups * slot, w), [], there, total)
                backs.append(cross(line.pin(out, label + "AB"[first > 0]), -dx))
            return backs

        def terms(first, groups, backs, kind):
            backs = [line.done(b) for b in backs]
            body = functools.partial(terms_kernel, first, nz, slot, len(backs))
            outs = [shape(tok, w, kind)] * groups
            return kernel_call("terms", body, outs, [], rank, taken, total, *backs)

        far_backs = across(nz - 1, 1) if nz > 1 else []
        if far_backs:
            yield
        near_backs = across(0, max(1, nz - 1))
        if near_backs:
            yield

        def far():
            return zring.halves(terms(nz - 1, 1, far_backs, BF)[0], tok // 2)

        def near():
            found = terms(0, max(1, nz - 1), near_backs, F32)
            return dict(zip(zring.offsets(), found))

        result = yield from zring.reduce(line, far, near)
        return result.astype(BF)

    if width % 128 == 0 and lanes >= 6:
        third = lanes // 3 * 128
        back_cuts = [width - 2 * third, third, third]
    else:
        back_cuts = [width]
    parts, lo = {}, 0
    for k, w in enumerate(back_cuts):
        parts["g%d" % k] = give(lo, lo + w, "g%d" % k)
        lo += w
    def weights(left, right):
        yield
        return line.done(unpick(line.go(left), right).astype(BF))

    parts["u"], parts["w"] = weights(d_hidden, inputs), weights(act, routed)
    order = BACK if (nz, nx, ny, nc, len(parts)) == (4, 2, 2, 2, 5) else []
    got = {}
    run(parts, order, got)
    results = [got["g%d" % k] for k in range(len(back_cuts))]
    grad_up, grad_down = got["u"].T, got["w"]
    token_grad = jnp.concatenate(results, axis=1)
    return (token_grad, grad_up[None], grad_down[None])


def solution(mesh):
    placed = (
        P("exp", "tp"),
        P("exp", "tp"),
        P("exp", None, "tp"),
        P("exp", "tp", None),
        P("exp", None),
        P("exp", None),
    )
    return jax.shard_map(
        per_device,
        mesh=mesh,
        in_specs=placed,
        out_specs=(P("exp", "tp"), P("exp", None, "tp"), P("exp", "tp", None)),
        check_vma=False,
    )
```
